128 devices in a mesh: trow: 4 (over z), tcol: 32 (over y, x, core).
Axes of the slice: x: 4, y: 4, z: 4, core: 2. Of those that a mesh axis runs over, the one named last changes fastest.
Arguments:
- object_slab: float32 [2, 4096, 32768], P(None, 'trow', 'tcol'), may hold values from -6 to 6
- probe_field: float32 [2, 256, 256], replicated, may hold values from -6 to 6
- amplitudes: bfloat16 [2048, 256, 256], P(('trow', 'tcol')), may hold values from 0.19921875 to 3
- positions: int32 [2048, 2], P(('trow', 'tcol')), may hold values from 0 to 1023
- shift_bins: int32 [2048, 2], P(('trow', 'tcol')), may hold values from 0 to 15
- destinations: int32 [2048, 1], P(('trow', 'tcol')), may hold values from 0 to 31; in each aligned block of 16 rows (0 to 15, 16 to 31, ...) at most 2 rows name the same one
- frame_counts: int32 [128], P(('trow', 'tcol')), may hold values from 1 to 16
Outputs:
- probe_step: float32 [2, 256, 256], replicated
- arrivals: float32 [8192, 3], P(('trow', 'tcol'))
The draws below stay inside these ranges and needn't reach their ends.
Inputs may be any that keep to these rules, and one draw needn't show every extreme that they name: `destinations`: among the slots of one device at most 2 share a destination, and in some device exactly 2 do.
All inputs are finite; a program needn't handle non-finite values.
Results may differ from the reference program's by a relative error of at most 0.0003.
Values sent between devices are 32-bit elements; how exact they have to be, the bound alone decides.
No kernel may reach another device: no remote copies, remote signals or barrier semaphores. Data moves between devices by JAX's collectives and lax.ppermute only.
A program may use at most 128 MiB of HBM per device.

```python
import math
import jax
import jax.numpy as jnp
import numpy as np
from jax import lax

TILE = 1024
FRAME = 256
HALF = 128
FRAMES_DEV = 16
BINS = 16
CAP = 2
FRAMES = 2048
NROW = 4096
NCOL = 32768
N_TCOL = 32
DEVICES = 128


def place_ends(array, own_key, least, high):
    dims = array.shape
    place = [jax.random.randint(jax.random.fold_in(own_key, axis), (), 0, dims[axis]) for axis in range(len(dims))]
    array = array.at[tuple(place)].set(least)
    longest = dims.index(max(dims))
    place[longest] = (place[longest] + 1) % dims[longest]
    return array.at[tuple(place)].set(high)


def block_levels(own_key, extent, pieces, low, high):
    loudness = 1.0
    for axis_at, parts in pieces:
        heights = jax.random.uniform(jax.random.fold_in(jax.random.fold_in(own_key, 6), axis_at), (parts,), jnp.float32, low / len(pieces), high / len(pieces))
        loudness = loudness * jnp.repeat(jnp.exp(heights), extent[axis_at] // parts).reshape((-1,) + (1,) * (len(extent) - 1 - axis_at))
    return loudness


def shared_out(key, own, number, rows, number_of, top, reach, slope):
    sequence = jax.random.permutation(key, number_of)
    crowded, usual = shares(number_of, rows * top, reach, slope, True), shares(number_of, rows * top, reach, slope, False)
    places = jnp.arange(number_of)

    def named(lengths, offset_by):
        used = int((lengths > 0).sum())
        fixed = max(1, used // 4)
        passed = fixed + (places - fixed + offset_by * (used - fixed)) % max(1, number_of - fixed)
        return jnp.zeros((number_of,), jnp.int32).at[sequence[jnp.where(places < fixed, places, passed)]].set(jnp.asarray(lengths, jnp.int32))

    lengths = jnp.where(number % 4 == 0, named(crowded, number // 4), named(usual, number - number // 4 - 1))
    mixed = jax.random.permutation(jax.random.fold_in(own, 3), number_of)
    donor, taker = mixed[0:number_of // 2 * 2:2], mixed[1:number_of // 2 * 2:2]
    margin = jnp.minimum(lengths[donor] - 1, reach - lengths[taker]) // 2
    margin = jnp.where((donor == sequence[0]) | (taker == sequence[0]) | (lengths[taker] == 0), 0, jnp.maximum(margin, 0))
    passed = jax.random.randint(jax.random.fold_in(own, 4), (number_of // 2,), 0, 1 << 20) % (margin + 1)
    lengths = lengths.at[donor].add(-passed).at[taker].add(passed)
    items = jnp.searchsorted(jnp.cumsum(lengths), jnp.arange(rows * top), side="right").astype(jnp.int32)
    table = items.reshape(top, rows).T
    table = table[jax.random.permutation(jax.random.fold_in(own, 1), rows)]
    offset_by = jax.random.randint(jax.random.fold_in(own, 2), (rows, 1), 0, top)
    return jnp.take_along_axis(table, (jnp.arange(top)[None, :] + offset_by) % top, axis=1)


def shares(number_of, total, most, lean, full):
    portions = [(1 << 20) // math.isqrt(standing ** lean) + 1 for standing in range(1, number_of + 1)]
    largest = most if full else min(most, max(-(-total // number_of), total * portions[0] // sum(portions)))
    least = 1 if total - largest >= number_of - 1 else 0
    given, rest = [largest] + [least] * (number_of - 1), total - largest - least * (number_of - 1)
    while rest > 0:
        movable = [i for i in range(1, number_of) if given[i] < largest] or [i for i in range(1, number_of) if given[i] < most]
        whole, remaining = sum([portions[i] for i in movable]), rest
        for i in movable:
            more = min(most - given[i], max(1, remaining * portions[i] // whole), rest)
            given[i] = given[i] + more
            rest = rest - more
    return np.array(given)


def scatter_about(key, dims, width, reach, cuts=(), dtype=jnp.bfloat16):
    values = jax.random.normal(key, dims, jnp.float32) * width
    if len(cuts) > 0:
        values = block_levels(key, dims, cuts, -0.22, 0.18) * values
    return jnp.clip(values, min=-reach, max=reach).astype(dtype)


def setup_inputs(seed: int = 0) -> dict:
    arg_keys = jax.random.split(jax.random.key(seed), 8)
    object_slab = scatter_about(arg_keys[0], (2, NROW, NCOL), 1.0, 6.0, ((1, 4), (2, 32)), jnp.float32)
    probe_field = scatter_about(arg_keys[1], (2, FRAME, FRAME), 1.0, 6.0, (), jnp.float32)
    amplitudes = jnp.clip(jnp.exp(math.log(3.0) - 2.7119641 * jax.random.uniform(arg_keys[2], (FRAMES, FRAME, FRAME), jnp.float32) ** block_levels(arg_keys[2], (FRAMES, FRAME, FRAME), ((0, 128),), -0.2, 0.2)), 0.19921875, 3.0).astype(jnp.bfloat16)
    positions = place_ends(jax.random.randint(arg_keys[3], (FRAMES, 2), 0, TILE), jax.random.fold_in(arg_keys[3], 1), 0, TILE - 1).astype(jnp.int32)
    shift_bins = place_ends(jax.random.randint(arg_keys[4], (FRAMES, 2), 0, BINS), jax.random.fold_in(arg_keys[4], 1), 0, BINS - 1).astype(jnp.int32)
    destinations_keys = jax.random.split(jax.random.fold_in(arg_keys[5], 1), FRAMES // FRAMES_DEV)
    destinations_turns = jax.random.permutation(jax.random.fold_in(arg_keys[5], 3), FRAMES // FRAMES_DEV)
    destinations = jax.vmap(lambda own, number: shared_out(jax.random.fold_in(arg_keys[5], 2), own, number, FRAMES_DEV, N_TCOL, 1, CAP, 2))(destinations_keys, destinations_turns).reshape((FRAMES, 1))
    frame_counts = place_ends(jax.random.randint(arg_keys[6], (DEVICES,), 1, FRAMES_DEV + 1), jax.random.fold_in(arg_keys[6], 1), 1, FRAMES_DEV).astype(jnp.int32)
    return dict(object_slab=object_slab, probe_field=probe_field, amplitudes=amplitudes, positions=positions, shift_bins=shift_bins, destinations=destinations, frame_counts=frame_counts)


def reference(object_slab, probe_field, amplitudes, positions, shift_bins, destinations, frame_counts):
    padded = jnp.pad(object_slab, ((0, 0), (HALF, HALF), (HALF, HALF)))
    wave_number = jnp.arange(FRAME)
    freqs = ((wave_number + HALF) % FRAME - HALF).astype(jnp.float32) / FRAME
    probe_wave = probe_field[0] + 1j * probe_field[1]
    frame_ids = jnp.arange(FRAMES)
    device = frame_ids // FRAMES_DEV
    tile_row = device // N_TCOL
    tile_col = device % N_TCOL
    live = (frame_ids % FRAMES_DEV < frame_counts[device]).astype(jnp.float32)

    def visit(carry, inputs):
        grad_real, grad_imag, weight = carry
        spot, bins_pair, measured, row_place, col_place, alive = inputs
        top = (row_place * TILE + spot[0]).astype(jnp.int32)
        left = (col_place * TILE + spot[1]).astype(jnp.int32)
        patch = lax.dynamic_slice(padded, (jnp.zeros((), jnp.int32), top, left), (2, FRAME, FRAME))
        object_wave = patch[0] + 1j * patch[1]
        exit_wave = probe_wave * object_wave
        shifts = bins_pair.astype(jnp.float32) / BINS - 0.5
        theta = 2.0 * math.pi * (freqs[:, None] * shifts[0] + freqs[None, :] * shifts[1])
        ramp = jnp.cos(theta) - 1j * jnp.sin(theta)
        unshifted = jnp.fft.fft2(exit_wave, norm='ortho')
        spectrum = unshifted * ramp
        magnitude = jnp.sqrt(spectrum.real ** 2 + spectrum.imag ** 2 + 0.1)
        diff = measured.astype(jnp.float32) * spectrum / magnitude - spectrum
        error = jnp.sum(diff.real ** 2 + diff.imag ** 2) / (FRAME * FRAME)
        cross = diff.imag * unshifted.real - diff.real * unshifted.imag
        grad_y = 2.0 * math.pi / FRAME * jnp.sum(freqs[:, None] * cross)
        grad_x = 2.0 * math.pi / FRAME * jnp.sum(freqs[None, :] * cross)
        chi = jnp.fft.ifft2(diff * jnp.conj(ramp), norm='ortho')
        term = jnp.conj(object_wave) * chi
        new_carry = (grad_real + alive * term.real, grad_imag + alive * term.imag, weight + alive * (patch[0] ** 2 + patch[1] ** 2))
        return (new_carry, alive * jnp.stack([grad_y, grad_x, error]))
    zeros = jnp.zeros((FRAME, FRAME), jnp.float32)
    (grad_real, grad_imag, weight), records = lax.scan(visit, (zeros, zeros, zeros), (positions, shift_bins, amplitudes, tile_row, tile_col, live))
    probe_step = jnp.stack([grad_real, grad_imag]) / jnp.sqrt(weight + 1.0)[None]
    targets = destinations[:, 0].reshape(DEVICES, FRAMES_DEV)
    same = targets[:, :, None] == targets[:, None, :]
    slot_ids = jnp.arange(FRAMES_DEV)
    earlier = slot_ids[:, None] > slot_ids[None, :]
    rank = lax.optimization_barrier(jnp.sum((same & earlier[None]).astype(jnp.int32), axis=2)).reshape(FRAMES)
    rows = (((tile_row * N_TCOL + destinations[:, 0]) * N_TCOL + tile_col) * CAP + rank).astype(jnp.int32)
    arrivals = jnp.zeros((DEVICES * N_TCOL * CAP, 3), jnp.float32).at[rows].set(records)
    return (probe_step, arrivals)
```

```python
import math

import jax
import jax.numpy as jnp
import ml_dtypes
import numpy as np
from jax import lax
from jax.experimental import pallas as pl
from jax.experimental.pallas import tpu as pltpu
from jax.sharding import PartitionSpec as P

BINS = 16
FRAME = 256
HALF = 128
SLOTS = 16
TILE = 1024
PLANES = 3
BAND = 8


def two_parts(matrix):
    high = matrix.astype(ml_dtypes.bfloat16)
    low = (matrix - high.astype(np.float64)).astype(ml_dtypes.bfloat16)
    return high, low


def tables():
    n, j = np.arange(HALF)[:, None], np.arange(HALF)[None, :]

    def real_form(steps):
        angle = 2 * np.pi * (steps % FRAME) / FRAME
        c, s = np.cos(angle) / math.sqrt(FRAME), np.sin(angle) / math.sqrt(FRAME)
        return np.block([[c, -s], [s, c]])

    def on_right(matrix):
        high, low = two_parts(matrix)
        return np.concatenate([high, high, low], 0)

    def on_left(matrix):
        high, low = two_parts(matrix)
        return np.concatenate([high, high, low], 1)

    even, odd = real_form(2 * n * j), real_form(n * (2 * j + 1))
    rights = np.stack([on_right(even), on_right(odd), on_right(even.T), on_right(odd.T)])
    lefts = np.stack([on_left(even.T), on_left(odd.T), on_left(even), on_left(odd)])
    order = np.concatenate([np.arange(0, FRAME, 2), np.arange(1, FRAME, 2)])
    perm = np.zeros((FRAME, FRAME))
    perm[np.arange(FRAME), order] = 1
    perms = np.stack([perm, perm.T]).astype(ml_dtypes.bfloat16)
    freqs = ((order + HALF) % FRAME - HALF) / FRAME
    theta = 2 * np.pi * (np.arange(BINS) / BINS - 0.5)[:, None] * freqs[None, :]
    sine, cosine = np.sin(theta), np.cos(theta)
    rows = np.zeros((BINS, 16, FRAME))
    rows[:, 0], rows[:, 1], rows[:, 2], rows[:, 3] = freqs * sine, freqs * cosine, sine, cosine
    high, low = two_parts(rows)
    row_table = np.concatenate([high, high, low], 2)
    scale = -2 * np.pi / FRAME
    col_table = np.zeros((BINS, 16, FRAME), np.float32)
    col_table[:, 0], col_table[:, 1] = scale * cosine, scale * sine
    col_table[:, 2], col_table[:, 3] = scale * freqs * cosine, scale * freqs * sine
    return rights, lefts, perms, row_table, col_table


def halves(x):
    high = x.astype(jnp.bfloat16)
    return high, (x - high.astype(jnp.float32)).astype(jnp.bfloat16)


def dot(a, b):
    return jnp.dot(a, b, preferred_element_type=jnp.float32)


def right_apply(x, matrix):
    high, low = halves(x)
    return dot(jnp.concatenate([high, low, high], 1), matrix)


def left_apply(matrix, x):
    high, low = halves(x)
    return dot(matrix, jnp.concatenate([high, low, high], 0))


def beside(a, b):
    return jnp.concatenate([a, b], 1)


def above(a, b):
    return jnp.concatenate([a, b], 0)


def frame_step(refs, slot, row, col, g, row_bin, col_bin):
    window, measured, probe, rights, lefts, perms, row_table, col_table, patch, totals, sums = refs
    lane = lax.broadcasted_iota(jnp.int32, (FRAME, HALF), 1)
    inside = lane < HALF - col
    shift = lax.rem(HALF - col, HALF)
    for p in range(2):
        parts = [pltpu.roll(window[slot, j, p, pl.ds(row, FRAME), :], shift, 1) for j in range(3)]
        patch[p, :, :HALF] = jnp.where(inside, parts[0], parts[1])
        patch[p, :, HALF:] = jnp.where(inside, parts[1], parts[2])
    obj_real, obj_imag = patch[0], patch[1]
    wave_real = probe[0] * obj_real - probe[1] * obj_imag
    wave_imag = probe[0] * obj_imag + probe[1] * obj_real
    wr0, wr1, wi0, wi1 = wave_real[:, :HALF], wave_real[:, HALF:], wave_imag[:, :HALF], wave_imag[:, HALF:]
    even = right_apply(beside(wr0 + wr1, wi0 + wi1), rights[0])
    odd = right_apply(beside(wr0 - wr1, wi0 - wi1), rights[1])
    mid_real, mid_imag = beside(even[:, :HALF], odd[:, :HALF]), beside(even[:, HALF:], odd[:, HALF:])
    mr0, mr1, mi0, mi1 = mid_real[:HALF], mid_real[HALF:], mid_imag[:HALF], mid_imag[HALF:]
    spectra = (
        left_apply(lefts[0], above(mr0 + mr1, mi0 + mi1)),
        left_apply(lefts[1], above(mr0 - mr1, mi0 - mi1)),
    )
    ordered = dot(perms[0], dot(measured[slot], perms[1]).astype(jnp.bfloat16))
    weighted, back, error = [], [], 0.0
    for k, spectrum in enumerate(spectra):
        real, imag = spectrum[:HALF], spectrum[HALF:]
        power = real * real + imag * imag
        gain = ordered[HALF * k : HALF * (k + 1)] * lax.rsqrt(power + 0.1) - 1.0
        leaning = gain * power
        error = error + jnp.sum((leaning * gain).reshape(HALF // 8, 8, FRAME), axis=0)
        weighted.append(leaning)
        back.append(above(real * gain, imag * gain))
    moments = left_apply(row_table[row_bin], above(weighted[0], weighted[1]))
    sums[g, 0:8, :] = (moments * col_table[col_bin])[:8]
    sums[g, 8:16, :] = error
    first, second = left_apply(lefts[2], back[0]), left_apply(lefts[3], back[1])
    upper, lower = first + second, first - second
    chi_even, chi_odd = [
        right_apply(
            above(
                beside(upper[:HALF, cols], upper[HALF:, cols]),
                beside(lower[:HALF, cols], lower[HALF:, cols]),
            ),
            rights[2 + k],
        )
        for k, cols in enumerate((slice(0, HALF), slice(HALF, FRAME)))
    ]
    for j, chi in enumerate((chi_even + chi_odd, chi_even - chi_odd)):
        cols = slice(HALF * j, HALF * (j + 1))
        chi_real, chi_imag = chi[:, :HALF], chi[:, HALF:]
        o_real, o_imag = patch[0, :, cols], patch[1, :, cols]
        totals[0, :, cols] += o_real * chi_real + o_imag * chi_imag
        totals[1, :, cols] += o_real * chi_imag - o_imag * chi_real
        totals[2, :, cols] += o_real * o_real + o_imag * o_imag


def spread(core, destinations, sums, totals, keep, send, records, line):
    bands = FRAME // BAND // 2
    for out, half in ((keep, core), (send, 1 - core)):
        for k in range(bands):
            rows = pl.ds(pl.multiple_of(half * HALF + BAND * k, BAND), BAND)
            for p in range(PLANES):
                out[k, BAND * p : BAND * (p + 1), :] = totals[p, rows, :]
    grad_y = jnp.sum(sums[:, 0, :] + sums[:, 1, :], axis=1, keepdims=True)
    grad_x = jnp.sum(sums[:, 2, :] + sums[:, 3, :], axis=1, keepdims=True)
    error = jnp.sum(jnp.sum(sums[:, 8:16, :], axis=1), axis=1, keepdims=True) / (FRAME * FRAME)
    lane = lax.broadcasted_iota(jnp.int32, (SLOTS, HALF), 1)
    line[...] = jnp.where(lane == 0, grad_y, jnp.where(lane == 1, grad_x, jnp.where(lane == 2, error, 0.0)))
    records[...] = jnp.zeros_like(records)

    def place(g, _):
        target = destinations[g, 0]
        rank = lax.fori_loop(0, g, lambda i, n: n + (destinations[i, 0] == target).astype(jnp.int32), jnp.int32(0))
        records[target, pl.ds(rank, 1), :] = line[pl.ds(g, 1), :]
        return 0

    lax.fori_loop(0, SLOTS, place, 0)


def frames_kernel(row_edge, col_edge):
    first, last = not (row_edge or col_edge), row_edge and col_edge
    n_strips = 2 * (row_edge + col_edge + last)
    last_rows = TILE - 2 * HALF

    def kernel(*refs):
        refs = list(refs)
        positions, bins, counts = refs[:3]
        refs = refs[3:]
        if last:
            destinations, core = refs[:2]
            refs = refs[2:]
        measured, probe, rights, lefts, perms, row_table, col_table, tile = refs[:8]
        refs = refs[8:]
        if not first:
            totals_in, sums_in = refs[:2]
            strips = refs[2 : 2 + n_strips]
            refs = refs[2 + n_strips :]
        if last:
            keep, send, records, totals, sums, line = refs[:6]
            refs = refs[6:]
        else:
            totals, sums = refs[:2]
            refs = refs[2:]
        window, buffer, patch, todo, sems = refs

        def choose(g, n):
            r, c = positions[g, 0], positions[g, 1]
            row_out = (r < HALF) | (r >= TILE - HALF)
            col_out = (c < HALF) | (c >= TILE - HALF)
            wanted = (g < counts[0]) & (row_out == row_edge) & (col_out == col_edge)

            @pl.when(wanted)
            def _():
                todo[n] = g

            return n + wanted.astype(jnp.int32)

        n = lax.fori_loop(0, SLOTS, choose, jnp.int32(0))

        def copies(i):
            g = todo[i]
            slot = lax.rem(i, 2)
            r, c = positions[g, 0], positions[g, 1]
            on_top, on_left = r < HALF, c < HALF
            choices = []

            def add(cond, ref, row, col, length, dst, j, sem):
                col = pl.multiple_of(col, HALF)
                return cond, pltpu.make_async_copy(
                    ref.at[:, pl.ds(row, length), pl.ds(col, HALF)], window.at[slot, j, :, pl.ds(dst, length)], sems.at[slot, sem]
                )

            if row_edge:
                ends = strips[-4:-2] if last else strips
                mid_row = pl.multiple_of(jnp.where(on_top, 0, last_rows), HALF)
                mid_dst = pl.multiple_of(jnp.where(on_top, HALF, 0), HALF)
                end_dst = pl.multiple_of(jnp.where(on_top, 0, 2 * HALF), HALF)
                corner = jnp.where(on_top, 0, 1)
                length = 2 * HALF
            else:
                mid_row, mid_dst, length = pl.multiple_of(((r - HALF) // 8) * 8, 8), 0, FRAME + 8
            if col_edge:
                sides = strips[:2]
                corners = strips[-2:]
            for j in range(3):
                if not col_edge:
                    options = [(None, None, ((c - HALF) // HALF) * HALF + HALF * j)]
                elif j == 1:
                    options = [(None, None, jnp.where(on_left, 0, TILE - HALF))]
                elif j == 0:
                    options = [(on_left, 0, 0), (jnp.logical_not(on_left), None, last_rows)]
                else:
                    options = [(on_left, None, HALF), (jnp.logical_not(on_left), 1, 0)]
                choices.append(
                    [add(cond, tile if side is None else sides[side], mid_row, col, length, mid_dst, j, j) for cond, side, col in options]
                )
                if row_edge:
                    found = []
                    for cond, side, col in options:
                        if side is None:
                            for here, ref in ((on_top, ends[0]), (jnp.logical_not(on_top), ends[1])):
                                here = here if cond is None else here & cond
                                found.append(add(here, ref, 0, col, HALF, end_dst, j, 3 + j))
                        else:
                            found.append(add(cond, corners[side].at[corner], 0, 0, HALF, end_dst, j, 3 + j))
                    choices.append(found)
            choices.append([(None, pltpu.make_async_copy(measured.at[g], buffer.at[slot], sems.at[slot, 6]))])
            return choices

        def start(i):
            for options in copies(i):
                for cond, copy in options:
                    if cond is None:
                        copy.start()
                    else:
                        pl.when(cond)(copy.start)

        @pl.when(n > 0)
        def _():
            start(0)

        if first:
            totals[...] = jnp.zeros_like(totals)
            sums[...] = jnp.zeros_like(sums)
        else:
            totals[...] = totals_in[...]
            sums[...] = sums_in[...]

        def step(i, _):
            @pl.when(i + 1 < n)
            def _():
                start(i + 1)

            for options in copies(i):
                options[0][1].wait()
            g = todo[i]
            r, c = positions[g, 0], positions[g, 1]
            frame_step(
                (window, buffer, probe, rights, lefts, perms, row_table, col_table, patch, totals, sums),
                lax.rem(i, 2),
                jnp.where(r < HALF, r, r - (TILE - HALF)) if row_edge else lax.rem(r, 8),
                lax.rem(c, HALF),
                g,
                bins[g, 0],
                bins[g, 1],
            )
            return 0

        lax.fori_loop(0, n, step, 0)
        if last:
            spread(core[0], destinations, sums, totals, keep, send, records, line)

    return kernel


SMEM = pl.BlockSpec(memory_space=pltpu.SMEM)
VMEM = pl.BlockSpec(memory_space=pltpu.VMEM)
ANY = pl.BlockSpec(memory_space=pl.ANY)


def f32(*shape):
    return jax.ShapeDtypeStruct(shape, jnp.float32)


def frames_call(row_edge, col_edge, scalars, arrays, state=(), strips=(), extra=()):
    last = row_edge and col_edge
    bands = FRAME // BAND // 2
    totals_shape, sums_shape = (PLANES, FRAME, FRAME), (SLOTS, 16, FRAME)
    scratch = []
    if last:
        out_shape = [f32(bands, PLANES * BAND, FRAME)] * 2 + [f32(2 * bands, BAND, HALF)]
        scratch = [pltpu.VMEM(totals_shape, jnp.float32), pltpu.VMEM(sums_shape, jnp.float32), pltpu.VMEM((SLOTS, HALF), jnp.float32)]
    else:
        out_shape = [f32(*totals_shape), f32(*sums_shape)]
    rows = 3 * HALF if row_edge else FRAME + 8
    scratch += [
        pltpu.VMEM((2, 3, 2, rows, HALF), jnp.float32),
        pltpu.VMEM((2, FRAME, FRAME), jnp.bfloat16),
        pltpu.VMEM((2, FRAME, FRAME), jnp.float32),
        pltpu.SMEM((SLOTS,), jnp.int32),
        pltpu.SemaphoreType.DMA((2, 7)),
    ]
    scalars = [*scalars, *extra]
    return pl.pallas_call(
        frames_kernel(row_edge, col_edge),
        in_specs=[SMEM] * len(scalars) + [ANY] + [VMEM] * 6 + [ANY] + [VMEM] * len(state) + [ANY] * len(strips),
        out_specs=[VMEM] * len(out_shape),
        out_shape=out_shape,
        scratch_shapes=scratch,
        compiler_params=pltpu.CompilerParams(vmem_limit_bytes=32 * 1024 * 1024),
        cost_estimate=pl.CostEstimate(flops=int(8e9), bytes_accessed=int(2e7), transcendentals=0),
    )(*scalars, *arrays, *state, *strips)


def step_kernel(summed, records, out):
    root = lax.rsqrt(summed[2 * BAND :, :] + 1.0)
    step = summed[: 2 * BAND, :] * jnp.concatenate([root, root], 0)
    for k in range(FRAME // BAND // 2):
        out[k, : 2 * BAND, :] = step
        out[k, 2 * BAND :, :HALF] = records[2 * k]
        out[k, 2 * BAND :, HALF:] = records[2 * k + 1]


def gather_kernel(core, mine, theirs, probe_step, arrivals, rows):
    odd = core[0] == 1
    bands = FRAME // BAND // 2
    for k in range(bands):
        own, far = mine[k], theirs[k]
        for half in range(2):
            part = jnp.where(odd == (half == 1), own, far)
            for p in range(2):
                probe_step[p, HALF * half + BAND * k : HALF * half + BAND * (k + 1), :] = part[BAND * p : BAND * (p + 1), :]
            record = part[2 * BAND : 2 * BAND + 2, :]
            rows[4 * k + 2 * half : 4 * k + 2 * half + 2, :] = jnp.where(odd, record[:, HALF:], record[:, :HALF])
    arrivals[...] = jnp.transpose(rows[...])[0:3, 0 : 4 * bands]


def body(object_slab, probe_field, amplitudes, positions, shift_bins, destinations, frame_counts):
    def shifted(array, axis, step):
        n = lax.axis_size(axis)
        return lax.ppermute(array, axis, [(i, i + step) for i in range(n) if 0 <= i + step < n])

    def across(array, axis, mask):
        return lax.ppermute(array, axis, [(i, i ^ mask) for i in range(lax.axis_size(axis))])

    def dealt(array):
        n = lax.axis_size("tcol")
        groups = [list(range(c, n, 2)) for c in range(2)]
        return lax.all_to_all(array, "tcol", 0, 0, axis_index_groups=groups, tiled=True)

    inner = TILE - HALF
    above_strip = shifted(object_slab[:, inner:, :], "trow", 1)
    below_strip = shifted(object_slab[:, :HALF, :], "trow", -1)
    left_strip = shifted(object_slab[:, :, inner:], "tcol", 1)
    right_strip = shifted(object_slab[:, :, :HALF], "tcol", -1)
    scalars = (positions, shift_bins, frame_counts)
    arrays = (amplitudes, probe_field, *(jnp.asarray(t) for t in tables()), object_slab)
    sides, ends = (left_strip, right_strip), (above_strip, below_strip)
    core = (lax.axis_index("tcol") % 2).astype(jnp.int32)[None]
    state = frames_call(False, False, scalars, arrays)
    state = frames_call(False, True, scalars, arrays, state, sides)
    stacked = jnp.stack(ends)
    corners = (shifted(stacked[:, :, :, inner:], "tcol", 1), shifted(stacked[:, :, :, :HALF], "tcol", -1))
    state = frames_call(True, False, scalars, arrays, state, ends)
    keep, send, records = frames_call(
        True, True, scalars, arrays, state, (*sides, *ends, *corners), (destinations, core)
    )
    summed = jnp.sum(dealt(keep + across(send, "tcol", 1)), axis=0)
    for mask in (1, 3):
        summed = summed + across(summed, "trow", mask)
    out = pl.pallas_call(
        step_kernel,
        in_specs=[VMEM, VMEM],
        out_specs=VMEM,
        out_shape=f32(FRAME // BAND // 2, PLANES * BAND, FRAME),
    )(summed, records)
    mine = dealt(out)
    probe_step, arrivals = pl.pallas_call(
        gather_kernel,
        in_specs=[SMEM, VMEM, VMEM],
        out_specs=[VMEM, VMEM],
        out_shape=[f32(2, FRAME, FRAME), f32(3, 2 * FRAME // BAND)],
        scratch_shapes=[pltpu.VMEM((HALF, HALF), jnp.float32)],
    )(core, mine, across(mine, "tcol", 1))
    return probe_step, arrivals.T


def solution(mesh):
    in_specs = (
        P(None, "trow", "tcol"),
        P(),
        P(("trow", "tcol"), None, None),
        P(("trow", "tcol"), None),
        P(("trow", "tcol"), None),
        P(("trow", "tcol"), None),
        P(("trow", "tcol")),
    )
    out_specs = (P(), P(("trow", "tcol"), None))
    return jax.shard_map(body, mesh=mesh, in_specs=in_specs, out_specs=out_specs, check_vma=False)
```

```python
import math

import jax
import jax.numpy as jnp
import ml_dtypes
import numpy as np
from jax import lax
from jax.experimental import pallas as pl
from jax.experimental.pallas import tpu as pltpu
from jax.sharding import PartitionSpec as P

BINS = 16
FRAME = 256
HALF = 128
SLOTS = 16
TILE = 1024
PLANES = 3
BAND = 8
CHUNK = 32
PAIR = 2
EARLY = 4
VMEM_LIMIT = 62 * 1024 * 1024


def two_parts(matrix):
    high = matrix.astype(ml_dtypes.bfloat16)
    low = (matrix - high.astype(np.float64)).astype(ml_dtypes.bfloat16)
    return high, low


def tables():
    n, j = np.arange(HALF)[:, None], np.arange(HALF)[None, :]

    def real_form(steps):
        angle = 2 * np.pi * (steps % FRAME) / FRAME
        c, s = np.cos(angle) / math.sqrt(FRAME), np.sin(angle) / math.sqrt(FRAME)
        return np.block([[c, -s], [s, c]])

    even, odd = real_form(2 * n * j), real_form(n * (2 * j + 1))
    mats = np.stack([part for matrix in (even, odd, even.T, odd.T) for part in two_parts(matrix)])
    order = np.concatenate([np.arange(0, FRAME, 2), np.arange(1, FRAME, 2)])
    perm = np.zeros((FRAME, FRAME))
    perm[np.arange(FRAME), order] = 1
    perms = np.stack([perm, perm.T]).astype(ml_dtypes.bfloat16)
    freqs = ((order + HALF) % FRAME - HALF) / FRAME
    theta = 2 * np.pi * (np.arange(BINS) / BINS - 0.5)[:, None] * freqs[None, :]
    sine, cosine = np.sin(theta), np.cos(theta)
    rows = np.zeros((BINS, 16, FRAME))
    rows[:, 0], rows[:, 1], rows[:, 2], rows[:, 3] = freqs * sine, freqs * cosine, sine, cosine
    high, low = two_parts(rows)
    high[:, 4:8] = low[:, 0:4]
    scale = -2 * np.pi / FRAME
    cols = np.zeros((BINS, 8, FRAME), np.float32)
    cols[:, 0], cols[:, 1], cols[:, 2], cols[:, 3] = cosine, sine, freqs * cosine, freqs * sine
    cols[:, 4:8] = cols[:, 0:4]
    return mats, perms, high, (scale * cols).astype(np.float32)


def dot(a, b):
    return jnp.dot(a, b, preferred_element_type=jnp.float32)


def put_halves(buffer, k, rows, x):
    high = x.astype(jnp.bfloat16)
    buffer[2 * k, rows, :] = high
    buffer[2 * k + 1, rows, :] = (x - high.astype(jnp.float32)).astype(jnp.bfloat16)


def right_apply(buffer, k, mats, i):
    high, low = buffer[2 * k], buffer[2 * k + 1]
    return dot(jnp.concatenate([high, low, high], 1), jnp.concatenate([mats[2 * i], mats[2 * i], mats[2 * i + 1]], 0))


def left_apply(mats, i, buffer, k):
    high, low = buffer[2 * k], buffer[2 * k + 1]
    return dot(jnp.concatenate([mats[2 * i], mats[2 * i], mats[2 * i + 1]], 1), jnp.concatenate([high, low, high], 0))


def beside(a, b):
    return jnp.concatenate([a, b], 1)


COLS = (slice(0, HALF), slice(HALF, FRAME))


def pieces(length):
    return [(slice(r, r + CHUNK), slice(HALF + r, HALF + r + CHUNK)) for r in range(0, length, CHUNK)]


def frame_steps(window, measured, fixed, work, sums, row, col, g, row_bin, col_bin):
    probe, mats, perms, row_table, col_table = fixed
    patch, parts, middle, ordered, leaning = work
    inside = lax.broadcasted_iota(jnp.int32, (CHUNK, HALF), 1) < HALF - col
    shift = lax.rem(HALF - col, HALF)
    ordered[...] = dot(perms[0], dot(measured[...], perms[1]).astype(jnp.bfloat16)).astype(jnp.bfloat16)
    for r in range(0, FRAME, CHUNK):
        rows = slice(r, r + CHUNK)
        planes = []
        for p in range(2):
            rolled = [pltpu.roll(window[j, p, pl.ds(row + r, CHUNK), :], shift, 1) for j in range(3)]
            planes.append([jnp.where(inside, rolled[0], rolled[1]), jnp.where(inside, rolled[1], rolled[2])])
        waves = []
        for j in range(2):
            real, imag = planes[0][j], planes[1][j]
            patch[0, rows, COLS[j]] = real
            patch[1, rows, COLS[j]] = imag
            p_real, p_imag = probe[0, rows, COLS[j]], probe[1, rows, COLS[j]]
            waves.append((p_real * real - p_imag * imag, p_real * imag + p_imag * real))
        (a_real, a_imag), (b_real, b_imag) = waves
        put_halves(parts, 0, rows, beside(a_real + b_real, a_imag + b_imag))
        put_halves(parts, 1, rows, beside(a_real - b_real, a_imag - b_imag))
    yield
    for k in range(2):
        middle[k] = right_apply(parts, k, mats, k)
    yield
    for top, bottom in pieces(HALF):
        for rows, cols in ((top, COLS[0]), (bottom, COLS[1])):
            upper = beside(middle[0, top, cols], middle[1, top, cols])
            lower = beside(middle[0, bottom, cols], middle[1, bottom, cols])
            put_halves(parts, 2, rows, upper + lower)
            put_halves(parts, 3, rows, upper - lower)
    yield
    for k in range(2):
        middle[k] = left_apply(mats, 2 + k, parts, 2 + k)
    yield
    error = 0.0
    for k in range(2):
        for top, bottom in pieces(HALF):
            real, imag = middle[k, top, :], middle[k, bottom, :]
            rows = slice(HALF * k + top.start, HALF * k + top.stop)
            power = real * real + imag * imag
            gain = ordered[rows, :].astype(jnp.float32) * lax.rsqrt(power + 0.1) - 1.0
            weighted = gain * power
            error = error + jnp.sum((weighted * gain).reshape(CHUNK // 8, 8, FRAME), axis=0)
            put_halves(leaning, 0, rows, weighted)
            put_halves(parts, k, top, real * gain)
            put_halves(parts, k, bottom, imag * gain)
    sums[g, 8:16, :] = error
    yield
    for k in range(2):
        middle[k] = left_apply(mats, k, parts, k)
    moments = dot(row_table[row_bin], leaning[0]) + dot(row_table[row_bin], leaning[1])
    sums[g, 0:8, :] = moments[:8] * col_table[col_bin]
    yield
    for top, bottom in pieces(HALF):
        for k, cols in enumerate(COLS):
            even = beside(middle[0, top, cols], middle[0, bottom, cols])
            odd = beside(middle[1, top, cols], middle[1, bottom, cols])
            put_halves(parts, 2 + k, top, even + odd)
            put_halves(parts, 2 + k, bottom, even - odd)
    yield
    for k in range(2):
        middle[k] = right_apply(parts, 2 + k, mats, 2 + k)


def add_terms(works, totals):
    for r in range(0, FRAME, CHUNK):
        rows = slice(r, r + CHUNK)
        for j, cols in enumerate(COLS):
            added = [totals[p, rows, cols] for p in range(PLANES)]
            for patch, _, middle, _, _ in works:
                even, odd = middle[0, rows, :], middle[1, rows, :]
                chi = even + odd if j == 0 else even - odd
                chi_real, chi_imag = chi[:, :HALF], chi[:, HALF:]
                real, imag = patch[0, rows, cols], patch[1, rows, cols]
                added[0] += real * chi_real + imag * chi_imag
                added[1] += real * chi_imag - imag * chi_real
                added[2] += real * real + imag * imag
            for p in range(PLANES):
                totals[p, rows, cols] = added[p]


def spread(core, destinations, all_sums, all_totals, keep, send, records, line, held, taken):
    bands = FRAME // BAND // 2
    for out, half in ((keep, core), (send, 1 - core)):
        for k in range(bands):
            rows = pl.ds(pl.multiple_of(half * HALF + BAND * k, BAND), BAND)
            for p in range(PLANES):
                out[k, BAND * p : BAND * (p + 1), :] = sum(totals[p, rows, :] for totals in all_totals)
    sums = sum(part[...] for part in all_sums)
    grad_y = jnp.sum(sums[:, 0, :] + sums[:, 1, :] + sums[:, 4, :] + sums[:, 5, :], axis=1, keepdims=True)
    grad_x = jnp.sum(sums[:, 2, :] + sums[:, 3, :] + sums[:, 6, :] + sums[:, 7, :], axis=1, keepdims=True)
    error = jnp.sum(jnp.sum(sums[:, 8:16, :], axis=1), axis=1, keepdims=True) / (FRAME * FRAME)
    lane = lax.broadcasted_iota(jnp.int32, (SLOTS, HALF), 1)
    line[...] = jnp.where(lane == 0, grad_y, jnp.where(lane == 1, grad_x, jnp.where(lane == 2, error, 0.0)))
    held[...] = jnp.zeros_like(held)

    for k in range(2 * bands):
        taken[k] = 0
    for g in range(SLOTS):
        target = destinations[0, g]
        rank = taken[target]
        taken[target] = rank + 1
        held[target, pl.ds(rank, 1), :] = line[g : g + 1, :]
    for k in range(bands):
        records[k] = beside(held[2 * k], held[2 * k + 1])


def frames_kernel(stage):
    first, last = stage == 0, stage == 2
    row_edge = last
    n_strips = 6 if last else 0 if first else 2

    def kernel(*refs):
        refs = list(refs)

        def take(count):
            taken = refs[:count]
            del refs[:count]
            return taken

        positions, bins, counts = take(3)
        if not first:
            (odds,) = take(1)
        if last:
            (destinations,) = take(1)
        measured, tile = take(2)
        tables_in = take(5)
        strips = take(n_strips)
        if last:
            earlier = take(4)
            keep, send, records, totals, sums, line, placed, taken = take(8)
            held = take(4)
        else:
            totals, sums = take(2)
        window, buffer, todo, sems, table_sems = take(5)
        fixed = take(5)
        work = refs

        def choose(g, carry):
            n, seen = carry
            r, c = positions[0, g], positions[1, g]
            row_out = (r < HALF) | (r >= TILE - HALF)
            wanted = (g < counts[0]) & (row_out == row_edge)
            if not row_edge:
                free = wanted & (c >= HALF) & (c < TILE - HALF)
                early = free & (seen < EARLY)
                seen = seen + free.astype(jnp.int32)
                wanted = early if first else wanted & jnp.logical_not(early)
            todo[n] = g
            return n + wanted.astype(jnp.int32), seen

        n, _ = lax.fori_loop(0, SLOTS, choose, (jnp.int32(0), jnp.int32(0)), unroll=True)

        def copies(i):
            g = todo[i]
            slot = lax.rem(i, 2 * PAIR)
            r, c = positions[0, g], positions[1, g]
            on_top, on_left, on_right = r < HALF, c < HALF, c >= TILE - HALF
            off_left, off_right = c >= HALF, c < TILE - HALF
            if not first:
                col_side = [on_left == (odds[0] == 1), on_left != (odds[0] == 1)]
                row_side = [on_top == (odds[1] == 1), on_top != (odds[1] == 1)]
            left = (c // HALF - 1) * HALF

            def option(cond, ref, row, col, length, dst, j, sem):
                source = ref.at[:, pl.ds(row, length), pl.ds(pl.multiple_of(col, HALF), HALF)]
                return cond, source, window.at[slot, j, :, pl.ds(dst, length)], sems.at[slot, sem]

            if row_edge:
                mid_row = pl.multiple_of(jnp.where(on_top, 0, TILE - 2 * HALF), HALF)
                mid_dst = pl.multiple_of(jnp.where(on_top, HALF, 0), HALF)
                end_dst = pl.multiple_of(jnp.where(on_top, 0, 2 * HALF), HALF)
                length = 2 * HALF
            else:
                mid_row, mid_dst, length = pl.multiple_of((r // 8) * 8 - HALF, 8), 0, FRAME + 8
            found = []
            for j in range(3):
                col = jnp.clip(left + HALF * j, 0, TILE - HALF)
                if first or j == 1:
                    found.append([option(None, tile, mid_row, col, length, mid_dst, j, j)])
                else:
                    beyond, within = (on_left, off_left) if j == 0 else (on_right, off_right)
                    options = [option(within, tile, mid_row, col, length, mid_dst, j, j)]
                    for w in range(2):
                        options.append(option(beyond & col_side[w], strips[w], mid_row, 0, length, mid_dst, j, j))
                    found.append(options)
                if row_edge:
                    options = []
                    for v in range(2):
                        here = row_side[v]
                        if j == 1:
                            options.append(option(here, strips[2 + v], 0, col, HALF, end_dst, j, 3 + j))
                        else:
                            options.append(option(here & within, strips[2 + v], 0, col, HALF, end_dst, j, 3 + j))
                            for w in range(2):
                                corner = strips[4 + v].at[w]
                                options.append(option(here & beyond & col_side[w], corner, 0, 0, HALF, end_dst, j, 3 + j))
                    found.append(options)
            found.append([(None, measured.at[g], buffer.at[slot], sems.at[slot, 6])])
            return found

        def start(i):
            @pl.when(i < n)
            def _():
                for options in copies(i):
                    for cond, *ends in options:
                        if cond is None:
                            pltpu.make_async_copy(*ends).start()
                        else:
                            pl.when(cond)(pltpu.make_async_copy(*ends).start)

        for u in range(PAIR):
            start(u)
        loads = [pltpu.make_async_copy(src, dst, table_sems.at[k]) for k, (src, dst) in enumerate(zip(tables_in, fixed))]
        for load in loads:
            load.start()
        if last:
            recalls = [pltpu.make_async_copy(src, dst, table_sems.at[5 + k]) for k, (src, dst) in enumerate(zip(earlier, held))]
            for recall in recalls:
                recall.start()
        totals[...] = jnp.zeros_like(totals)
        sums[...] = jnp.zeros_like(sums)
        for load in loads:
            load.wait()

        def together(i, count):
            for u in range(count):
                for options in copies(PAIR * i + u):
                    pltpu.make_async_copy(*options[0][1:]).wait()
            works, runs = [], []
            for u in range(count):
                k = PAIR * i + u
                g, slot = todo[k], lax.rem(k, 2 * PAIR)
                r, c = positions[0, g], positions[1, g]
                works.append([ref.at[u] for ref in work])
                row = jnp.where(r < HALF, r, r - (TILE - HALF)) if row_edge else lax.rem(r, 8)
                runs.append(
                    frame_steps(
                        window.at[slot], buffer.at[slot], fixed, works[u], sums, row, lax.rem(c, HALF), g, bins[0, g], bins[1, g]
                    )
                )
            while runs:
                runs = [run for run in runs if next(run, runs) is None]
            add_terms(works, totals)

        def step(i, _):
            for u in range(PAIR):
                start(PAIR * (i + 1) + u)
            together(i, PAIR)
            return 0

        full = n // PAIR
        lax.fori_loop(0, full, step, 0)
        for count in range(1, PAIR):
            pl.when(n - PAIR * full == count)(lambda: together(full, count))
        if last:
            for recall in recalls:
                recall.wait()
            spread(odds[0], destinations, (sums, held[1], held[3]), (totals, held[0], held[2]), keep, send, records, line, placed, taken)

    return kernel


SMEM = pl.BlockSpec(memory_space=pltpu.SMEM)
VMEM = pl.BlockSpec(memory_space=pltpu.VMEM)
HBM = pl.BlockSpec(memory_space=pltpu.HBM)
ANY = pl.BlockSpec(memory_space=pl.ANY)


def f32(*shape):
    return jax.ShapeDtypeStruct(shape, jnp.float32)


def frames_call(stage, scalars, sources, fixed, strips=(), earlier=(), extra=()):
    last = stage == 2
    bands = FRAME // BAND // 2
    totals_shape, sums_shape = (PLANES, FRAME, FRAME), (SLOTS, 16, FRAME)
    scratch = []
    if last:
        out_shape = [f32(bands, PLANES * BAND, FRAME)] * 2 + [f32(bands, BAND, FRAME)]
        scratch = [pltpu.VMEM(totals_shape, jnp.float32), pltpu.VMEM(sums_shape, jnp.float32), pltpu.VMEM((SLOTS, HALF), jnp.float32)]
        scratch += [pltpu.VMEM((2 * bands, BAND, HALF), jnp.float32), pltpu.SMEM((2 * bands,), jnp.int32)]
        scratch += [pltpu.VMEM(shape, jnp.float32) for shape in (totals_shape, sums_shape) * 2]
    else:
        out_shape = [f32(*totals_shape), f32(*sums_shape)]
    rows = 3 * HALF if last else FRAME + 8
    scratch += [
        pltpu.VMEM((2 * PAIR, 3, 2, rows, HALF), jnp.float32),
        pltpu.VMEM((2 * PAIR, FRAME, FRAME), jnp.bfloat16),
        pltpu.SMEM((SLOTS + 1,), jnp.int32),
        pltpu.SemaphoreType.DMA((2 * PAIR, 7)),
        pltpu.SemaphoreType.DMA((9,)),
        *(pltpu.VMEM(t.shape, t.dtype) for t in fixed),
        pltpu.VMEM((PAIR, 2, FRAME, FRAME), jnp.float32),
        pltpu.VMEM((PAIR, 8, FRAME, FRAME), jnp.bfloat16),
        pltpu.VMEM((PAIR, 2, FRAME, FRAME), jnp.float32),
        pltpu.VMEM((PAIR, FRAME, FRAME), jnp.bfloat16),
        pltpu.VMEM((PAIR, 2, FRAME, FRAME), jnp.bfloat16),
    ]
    scalars = [*scalars, *extra]
    return pl.pallas_call(
        frames_kernel(stage),
        in_specs=[SMEM] * len(scalars) + [ANY] * (7 + len(strips) + len(earlier)),
        out_specs=[VMEM] * len(out_shape),
        out_shape=out_shape,
        scratch_shapes=scratch,
        compiler_params=pltpu.CompilerParams(vmem_limit_bytes=VMEM_LIMIT),
        cost_estimate=pl.CostEstimate(flops=int(8e9), bytes_accessed=int(2e7), transcendentals=0),
    )(*scalars, *sources, *fixed, *strips, *earlier)


def strips_kernel(odds, tile, *refs):
    outs, held, sems = refs[:4], refs[4:8], refs[8]
    inner = TILE - HALF
    cols, rows = [[(pl.multiple_of(jnp.where(odds[k] == side, inner, 0), HALF), HALF) for side in (0, 1)] for k in (0, 1)]
    whole = (0, TILE)
    boxes = [(r, whole) for r in rows] + [(whole, c) for c in cols]
    loads = [
        pltpu.make_async_copy(tile.at[:, pl.ds(*r), pl.ds(*c)], here, sems.at[0, k])
        for k, ((r, c), here) in enumerate(zip(boxes, held))
    ]
    stores = [pltpu.make_async_copy(here, out, sems.at[1, k]) for k, (here, out) in enumerate(zip(held, outs))]
    for load in loads:
        load.start()
    for load, store in zip(loads, stores):
        load.wait()
        store.start()
    for store in stores:
        store.wait()


def strips_call(odds, tile):
    shapes = [(2, HALF, TILE)] * 2 + [(2, TILE, HALF)] * 2
    return pl.pallas_call(
        strips_kernel,
        in_specs=[SMEM, ANY],
        out_specs=[ANY] * 4,
        out_shape=[f32(*shape) for shape in shapes],
        scratch_shapes=[pltpu.VMEM(shape, jnp.float32) for shape in shapes] + [pltpu.SemaphoreType.DMA((2, 4))],
        compiler_params=pltpu.CompilerParams(vmem_limit_bytes=VMEM_LIMIT),
    )(odds, tile)


def body(object_slab, probe_field, amplitudes, positions, shift_bins, destinations, frame_counts):
    cols = lax.axis_size("tcol")

    def swapped(array, axis, side):
        n = lax.axis_size(axis)
        return lax.ppermute(array, axis, [pair for i in range(side, n - 1, 2) for pair in ((i, i + 1), (i + 1, i))])

    def across(array, axis, mask):
        return lax.ppermute(array, axis, [(i, i ^ mask) for i in range(lax.axis_size(axis))])

    def dealt(array):
        groups = [list(range(c, cols, 2)) for c in range(2)]
        return lax.all_to_all(array, "tcol", 0, 0, axis_index_groups=groups, tiled=True)

    odds = jnp.stack([lax.axis_index("tcol") % 2, lax.axis_index("trow") % 2]).astype(jnp.int32)
    sent = strips_call(odds, object_slab)
    rows = [swapped(sent[side], "trow", side) for side in range(2)]
    sides = [swapped(sent[2 + side], "tcol", side) for side in range(2)]
    scalars = (positions.T, shift_bins.T, frame_counts)
    sources = (amplitudes, object_slab)
    fixed = (probe_field, *(jnp.asarray(t) for t in tables()))
    begun = frames_call(0, scalars, sources, fixed)
    sides, begun = lax.optimization_barrier((sides, begun))
    both = jnp.stack(sides)
    low, high = both[:, :, TILE - HALF :], both[:, :, :HALF]
    corners = [swapped(jnp.where(odds[1] == side, low, high), "trow", side) for side in range(2)]
    between = frames_call(1, scalars, sources, fixed, sides, extra=(odds,))
    keep, send, records = frames_call(
        2, scalars, sources, fixed, (*sides, *rows, *corners), (*begun, *between), (odds, destinations.T)
    )
    summed = jnp.sum(dealt(keep + across(send, "tcol", 1)), axis=0)
    for mask in (1, 3):
        summed = summed + across(summed, "trow", mask)
    root = lax.rsqrt(summed[2 * BAND :] + 1.0)
    step = summed[: 2 * BAND] * jnp.concatenate([root, root], 0)
    out = jnp.concatenate([jnp.broadcast_to(step, (FRAME // BAND // 2, 2 * BAND, FRAME)), records], 1)
    mine = dealt(out)
    theirs = across(mine, "tcol", 1)
    odd = odds[0] == 1
    both = jnp.stack([jnp.where(odd, theirs, mine), jnp.where(odd, mine, theirs)])
    bands = FRAME // BAND // 2
    step = both[:, :, : 2 * BAND].reshape(2, bands, 2, BAND, FRAME)
    probe_step = jnp.transpose(step, (2, 0, 1, 3, 4)).reshape(2, FRAME, FRAME)
    record = both[:, :, 2 * BAND : 2 * BAND + 2]
    record = jnp.where(odd, record[..., HALF : HALF + 3], record[..., 0:3])
    return probe_step, jnp.transpose(record, (1, 0, 2, 3)).reshape(4 * bands, 3)


def solution(mesh):
    in_specs = (
        P(None, "trow", "tcol"),
        P(),
        P(("trow", "tcol"), None, None),
        P(("trow", "tcol"), None),
        P(("trow", "tcol"), None),
        P(("trow", "tcol"), None),
        P(("trow", "tcol")),
    )
    out_specs = (P(), P(("trow", "tcol"), None))
    return jax.shard_map(body, mesh=mesh, in_specs=in_specs, out_specs=out_specs, check_vma=False)
```
